32 devices in a mesh: seq: 8 (over z, y), head: 4 (over x, core).
Axes of the slice: x: 2, y: 2, z: 4, core: 2. Of those that a mesh axis runs over, the one named last changes fastest.
Arguments:
- hidden_in: bfloat16 [2, 4096, 1024], P(None, 'seq'), may hold values from -6 to 6
- norm_gain: bfloat16 [1024], replicated, may hold values from 0.099609375 to 1.8984375
- query_weight: bfloat16 [1024, 512], P(None, 'head'), may hold values from -0.1875 to 0.1875
- keyvalue_matrix: bfloat16 [1024, 2, 128], replicated, may hold values from -0.1875 to 0.1875
- output_weight: bfloat16 [512, 1024], P('head'), may hold values from -2 to 2
- zgate_weight: bfloat16 [1024, 1536], P(None, 'head'), may hold values from -0.1875 to 0.1875
- inner_weight: bfloat16 [1024, 1536], P(None, 'head'), may hold values from -0.1875 to 0.1875
- state_weight: bfloat16 [1024, 256], replicated, may hold values from -0.1875 to 0.1875
- step_weight: bfloat16 [1024, 24], P(None, 'head'), may hold values from -0.5 to 0.5
- conv_inner: bfloat16 [4, 1536], P(None, 'head'), may hold values from -3 to 3
- conv_state: bfloat16 [4, 256], replicated, may hold values from -3 to 3
- step_bias: float32 [24], P('head'), may hold values from -4 to 0.5
- decay_log: float32 [24], P('head'), may hold values from -4.5 to 0.5
- skip_gain: float32 [24], P('head'), may hold values from 0.5 to 4
- ssm_gain: bfloat16 [1536], P('head'), may hold values from 0.099609375 to 1.8984375
- mixer_weight: bfloat16 [1536, 1024], P('head'), may hold values from -0.15625 to 0.15625
- mlp_gain: bfloat16 [1024], replicated, may hold values from 0.099609375 to 1.8984375
- gate_weight: bfloat16 [1024, 2048], P(None, 'head'), may hold values from -0.1875 to 0.1875
- up_weight: bfloat16 [1024, 2048], P(None, 'head'), may hold values from -0.1875 to 0.1875
- down_weight: bfloat16 [2048, 1024], P('head'), may hold values from -0.125 to 0.125
- grad_output: bfloat16 [2, 4096, 1024], P(None, 'seq'), may hold values from -6 to 6
Outputs:
- output: bfloat16 [2, 4096, 1024], P(None, 'seq')
- grad_input: float32 [2, 4096, 1024], P(None, 'seq')
- grad_norm_gain: float32 [1024], replicated
- grad_query_weight: float32 [1024, 512], P(None, 'head')
- grad_keyvalue_weight: float32 [1024, 2, 128], replicated
- grad_output_weight: float32 [512, 1024], P('head')
- grad_zgate_weight: float32 [1024, 1536], P(None, 'head')
- grad_inner_weight: float32 [1024, 1536], P(None, 'head')
- grad_state_weight: float32 [1024, 256], replicated
- grad_step_weight: float32 [1024, 24], P(None, 'head')
- grad_conv_inner: float32 [4, 1536], P(None, 'head')
- grad_conv_state: float32 [4, 256], replicated
- grad_step_bias: float32 [24], P('head')
- grad_decay_log: float32 [24], P('head')
- grad_skip_gain: float32 [24], P('head')
- grad_ssm_gain: float32 [1536], P('head')
- grad_mixer_weight: float32 [1536, 1024], P('head')
- grad_mlp_gain: float32 [1024], replicated
- grad_gate_weight: float32 [1024, 2048], P(None, 'head')
- grad_up_weight: float32 [1024, 2048], P(None, 'head')
- grad_down_weight: float32 [2048, 1024], P('head')
The draws below stay inside these ranges and needn't reach their ends.
All inputs are finite; a program needn't handle non-finite values.
Results may differ from the reference program's by a relative error of at most 0.013.
The reference program's roundings to bfloat16 on the way count: a program that leaves them out, or rounds other values in their place, can miss the bound.
Values may be sent and summed in bfloat16 or wider, within the bound.
A program may use at most 256 MiB of HBM per device.

```python
import math
import jax
import jax.numpy as jnp
from jax import lax

D = 1024
HEADS = 8
KV_HEADS = 2
HEAD_DIM = 64
MHEADS = 24
MHEAD_DIM = 64
STATE = 128
FF = 2048
CONV = 4
SEQS = 2
SSM = 1536
LENGTH = 4096


def levels(stream_key, extent, shards, low, high):
    factor_of = 1.0
    for position, shards_of in shards:
        draws = jax.random.uniform(jax.random.fold_in(jax.random.fold_in(stream_key, 6), position), (shards_of,), jnp.float32, low / len(shards), high / len(shards))
        factor_of = factor_of * jnp.repeat(jnp.exp(draws), extent[position] // shards_of).reshape((-1,) + (1,) * (len(extent) - 1 - position))
    return factor_of


def noise(stream_key, extent, scale, most, cuts=(), kind=jnp.bfloat16):
    values = scale * jax.random.normal(stream_key, extent, jnp.float32)
    if cuts:
        values = values * levels(stream_key, extent, cuts, -0.22, 0.18)
    return jnp.clip(values, -most, most).astype(kind)


def setup_inputs(seed: int = 0) -> dict:
    arg_keys = jax.random.split(jax.random.key(seed), 22)
    return {
        "hidden_in": noise(arg_keys[0], (SEQS, LENGTH, D), 1.0, 6.0, ((1, 8),)),
        "norm_gain": jnp.clip(1.0 + 0.18 * jax.random.normal(arg_keys[1], (D,), jnp.float32), 0.099609375, 1.8984375).astype(jnp.bfloat16),
        "query_weight": noise(arg_keys[2], (D, HEADS * HEAD_DIM), D ** -0.5, 0.1875, ((1, 4),)),
        "keyvalue_matrix": noise(arg_keys[3], (D, KV_HEADS, 2 * HEAD_DIM), D ** -0.5, 0.1875),
        "output_weight": noise(arg_keys[4], (HEADS * HEAD_DIM, D), 8 ** -0.5, 2.0, ((0, 4),)),
        "zgate_weight": noise(arg_keys[5], (D, SSM), D ** -0.5, 0.1875, ((1, 4),)),
        "inner_weight": noise(arg_keys[6], (D, SSM), D ** -0.5, 0.1875, ((1, 4),)),
        "state_weight": noise(arg_keys[7], (D, 2 * STATE), D ** -0.5, 0.1875),
        "step_weight": noise(arg_keys[8], (D, MHEADS), (D // 8) ** -0.5, 0.5, ((1, 4),)),
        "conv_inner": noise(arg_keys[9], (CONV, SSM), CONV ** -0.5, 3.0, ((1, 4),)),
        "conv_state": noise(arg_keys[10], (CONV, 2 * STATE), CONV ** -0.5, 3.0),
        "step_bias": jnp.clip(-4.0 + 4.5 * jax.random.uniform(arg_keys[11], (MHEADS,), jnp.float32) ** levels(arg_keys[11], (MHEADS,), ((0, 4),), -0.2, 0.2), -4.0, 0.5),
        "decay_log": jnp.clip(-4.5 + 5.0 * jax.random.uniform(arg_keys[12], (MHEADS,), jnp.float32) ** levels(arg_keys[12], (MHEADS,), ((0, 4),), -0.2, 0.2), -4.5, 0.5),
        "skip_gain": jnp.clip(0.5 + 3.5 * jax.random.uniform(arg_keys[13], (MHEADS,), jnp.float32) ** levels(arg_keys[13], (MHEADS,), ((0, 4),), -0.2, 0.2), 0.5, 4.0),
        "ssm_gain": jnp.clip(1.0 + 0.18 * jax.random.normal(arg_keys[14], (SSM,), jnp.float32), 0.099609375, 1.8984375).astype(jnp.bfloat16),
        "mixer_weight": noise(arg_keys[15], (SSM, D), SSM ** -0.5, 0.15625, ((0, 4),)),
        "mlp_gain": jnp.clip(1.0 + 0.18 * jax.random.normal(arg_keys[16], (D,), jnp.float32), 0.099609375, 1.8984375).astype(jnp.bfloat16),
        "gate_weight": noise(arg_keys[17], (D, FF), D ** -0.5, 0.1875, ((1, 4),)),
        "up_weight": noise(arg_keys[18], (D, FF), D ** -0.5, 0.1875, ((1, 4),)),
        "down_weight": noise(arg_keys[19], (FF, D), FF ** -0.5, 0.125, ((0, 4),)),
        "grad_output": noise(arg_keys[20], (SEQS, LENGTH, D), 1.0, 6.0, ((1, 8),)),
    }


@jax.custom_vjp
def low(v):
    return lax.optimization_barrier(v.astype(jnp.bfloat16)).astype(jnp.float32)

@jax.custom_vjp
def low_back(v):
    return v

def low_keep(v):
    return (low(v), None)

def low_pass(kept, grad):
    return (grad,)

def back_keep(v):
    return (v, None)

def back_low(kept, grad):
    return (low(grad),)
low.defvjp(low_keep, low_pass)
low_back.defvjp(back_keep, back_low)
HIGH_ACCURACY = lax.Precision.HIGHEST
EPSILON = 1e-05
ROPE_BASE = 100000000000.0
MASKED = -1e+30

def rms_norm(values, gain):
    factor = lax.rsqrt(lax.optimization_barrier(jnp.mean(values * values, axis=-1, keepdims=True)) + EPSILON)
    return values * factor * gain

def project(left_operand, right_operand):
    return jnp.einsum('uog,gr->uor', left_operand, right_operand, precision=HIGH_ACCURACY)

def rotate(values, positions):
    half = values.shape[-1] // 2
    freq = ROPE_BASE ** (-jnp.arange(half, dtype=jnp.float32) * 2.0 / values.shape[-1])
    angle = positions[:, None] * freq[None, :]
    cosine = jnp.cos(angle)[None, :, None, :]
    sine = jnp.sin(angle)[None, :, None, :]
    first = values[..., :half]
    second = values[..., half:]
    return jnp.concatenate([first * cosine - second * sine, second * cosine + first * sine], axis=-1)

def conv_act(extended, conv_weight):
    rows = extended.shape[1] - (conv_weight.shape[0] - 1)
    summed = extended[:, 0:rows] * conv_weight[0]
    for tap in range(1, conv_weight.shape[0]):
        summed = summed + extended[:, tap:tap + rows] * conv_weight[tap]
    return jax.nn.silu(summed)

def ssm_inputs(extended, step_raw, conv_weight, step_bias, decay_log):
    activated = conv_act(extended, conv_weight)
    inner_width = activated.shape[-1] - 2 * STATE
    heads_here = step_raw.shape[-1]
    channels = activated[..., :inner_width].reshape(activated.shape[0], activated.shape[1], heads_here, inner_width // heads_here)
    writes = activated[..., inner_width:inner_width + STATE]
    reads = activated[..., inner_width + STATE:]
    step = jax.nn.softplus(step_raw + step_bias)
    logdecay = -step * jnp.exp(decay_log)
    return (channels, writes, reads, step, logdecay)

def intra(channels, writes, reads, step, running):
    rows = running.shape[1]
    lower = jnp.arange(rows, dtype=jnp.int32)[:, None] >= jnp.arange(rows, dtype=jnp.int32)[None, :]
    mask = lower[None, :, :, None]
    spread = running[:, :, None, :] - running[:, None, :, :]
    decay = jnp.where(mask, jnp.exp(jnp.where(mask, spread, 0.0)), 0.0)
    intersection = jnp.einsum('stn,sun->stu', reads, writes, precision=HIGH_ACCURACY)
    mixing = decay * intersection[..., None] * step[:, None, :, :]
    within = jnp.einsum('stuh,suhp->sthp', mixing, channels, precision=HIGH_ACCURACY)
    tail_weight = jnp.exp(running[:, -1:, :] - running) * step
    local = jnp.einsum('suh,suhp,sun->shpn', tail_weight, channels, writes, precision=HIGH_ACCURACY)
    return (within, local)

def inter(reads, running, state):
    return jnp.exp(running)[..., None] * jnp.einsum('stn,shpn->sthp', reads, state, precision=HIGH_ACCURACY)

def ssd_block(state, pieces):
    channels, writes, reads, step, logdecay = pieces
    running = jnp.cumsum(logdecay, axis=1)
    within, local = intra(channels, writes, reads, step, running)
    result = within + inter(reads, running, state)
    return (jnp.exp(running[:, -1])[:, :, None, None] * state + local, result)

def attention(queries, keys, values):
    seqs, length, heads, head_dim = queries.shape
    group = heads // keys.shape[2]
    keys_all = jnp.repeat(keys, group, axis=2)
    values_all = jnp.repeat(values, group, axis=2)
    query_block = math.gcd(length, 512)
    factor = head_dim ** (-0.5)
    key_pos = jnp.arange(length, dtype=jnp.int32)

    def one_block(start):
        block_q = lax.dynamic_slice_in_dim(queries, start, query_block, 1)
        scores = jnp.einsum('sqhd,skhd->shqk', block_q, keys_all, precision=HIGH_ACCURACY) * factor
        scores = low_back(scores)
        query_pos = start + jnp.arange(query_block, dtype=jnp.int32)
        allowed = key_pos[None, :] <= query_pos[:, None]
        scores = jnp.where(allowed[None, None], scores, MASKED)
        peak = lax.optimization_barrier(jnp.max(scores, axis=-1, keepdims=True))
        log_total = peak + jnp.log(lax.optimization_barrier(jnp.sum(jnp.exp(scores - peak), axis=-1, keepdims=True)))
        probs = low(jnp.exp(scores - log_total))
        return jnp.einsum('shqk,skhd->sqhd', probs, values_all, precision=HIGH_ACCURACY)
    starts = jnp.arange(length // query_block, dtype=jnp.int32) * query_block
    blocks = lax.map(jax.checkpoint(one_block), starts)
    return jnp.moveaxis(blocks, 0, 1).reshape(seqs, length, heads, head_dim)

def layer(hidden_in, norm_gain, query_weight, keyvalue_matrix, output_weight, zgate_weight, inner_weight, state_weight, step_weight, conv_inner, conv_state, step_bias, decay_log, skip_gain, ssm_gain, mixer_weight, mlp_gain, gate_weight, up_weight, down_weight):
    positions = jnp.arange(LENGTH, dtype=jnp.int32).astype(jnp.float32)
    normalized_input = low(rms_norm(hidden_in, norm_gain))
    query_raw = low_back(project(normalized_input, query_weight)).reshape(SEQS, LENGTH, HEADS, HEAD_DIM)
    queries = low(rotate(query_raw, positions))
    keyvalue_projected = low_back(jnp.einsum('cpf,fky->cpky', normalized_input, keyvalue_matrix, precision=HIGH_ACCURACY))
    keys = low(rotate(keyvalue_projected[..., :HEAD_DIM], positions))
    values = low(keyvalue_projected[..., HEAD_DIM:])
    attended = low_back(low(attention(queries, keys, values))).reshape(SEQS, LENGTH, HEADS * HEAD_DIM)
    zgate = low_back(project(normalized_input, zgate_weight))
    inner = low_back(jnp.concatenate([project(normalized_input, inner_weight), project(normalized_input, state_weight)], axis=-1))
    step_raw = low_back(project(normalized_input, step_weight))
    conv_weight = jnp.concatenate([conv_inner, conv_state], axis=1)
    extended = jnp.pad(inner, ((0, 0), (CONV - 1, 0), (0, 0)))
    channels, writes, reads, step, logdecay = ssm_inputs(extended, step_raw, conv_weight, step_bias, decay_log)
    block_len = math.gcd(LENGTH, 512)
    count = LENGTH // block_len

    def split(values_in):
        return jnp.moveaxis(values_in.reshape((SEQS, count, block_len) + values_in.shape[2:]), 1, 0)
    start_state = jnp.zeros((SEQS, MHEADS, MHEAD_DIM, STATE), jnp.float32)
    pieces = (split(channels), split(writes), split(reads), split(step), split(logdecay))
    final_state, y_blocks = lax.scan(jax.checkpoint(ssd_block), start_state, pieces)
    y_ssm = jnp.moveaxis(y_blocks, 0, 1).reshape(SEQS, LENGTH, MHEADS, MHEAD_DIM) + skip_gain[:, None] * channels
    gated = y_ssm.reshape(SEQS, LENGTH, SSM) * jax.nn.silu(zgate)
    ssm_normed = low(rms_norm(gated, ssm_gain))
    mixed = low_back(project(attended, output_weight) + project(ssm_normed, mixer_weight))
    hidden = hidden_in + mixed
    normed_two = low(rms_norm(hidden, mlp_gain))
    gate = low_back(project(normed_two, gate_weight))
    up = low_back(project(normed_two, up_weight))
    activated = low(jax.nn.silu(gate) * up)
    return hidden + project(activated, down_weight)

def reference(hidden_in, norm_gain, query_weight, keyvalue_matrix, output_weight, zgate_weight, inner_weight, state_weight, step_weight, conv_inner, conv_state, step_bias, decay_log, skip_gain, ssm_gain, mixer_weight, mlp_gain, gate_weight, up_weight, down_weight, grad_output):
    inputs = (hidden_in, norm_gain, query_weight, keyvalue_matrix, output_weight, zgate_weight, inner_weight, state_weight, step_weight, conv_inner, conv_state, step_bias, decay_log, skip_gain, ssm_gain, mixer_weight, mlp_gain, gate_weight, up_weight, down_weight)
    floats = [entry.astype(jnp.float32) for entry in inputs]
    result, pull = jax.vjp(layer, *floats)
    grads = pull(grad_output.astype(jnp.float32))
    return (result.astype(jnp.bfloat16), grads[0], grads[1], grads[2], grads[3], grads[4], grads[5], grads[6], grads[7], grads[8], grads[9], grads[10], grads[11], grads[12], grads[13], grads[14], grads[15], grads[16], grads[17], grads[18], grads[19])
```

```python
import math

import jax
import jax.numpy as jnp
from jax import lax
from jax.sharding import PartitionSpec as P

HEADS = 8
KV_HEADS = 2
STATE = 128
SSM = 1536


HIGH_ACCURACY = lax.Precision.HIGHEST
EPSILON = 1e-05
ROPE_BASE = 100000000000.0
MASKED = -1e30


def passed_along(value, axis, steps):
    count = lax.axis_size(axis)
    first, last = (max(0, -steps), min(count, count - steps))
    return lax.ppermute(value, axis, [(source, source + steps) for source in range(first, last)])


def carried(log_totals, states, axis, backward):
    count, mine = (lax.axis_size(axis), lax.axis_index(axis))
    pieces = lax.all_gather(states.astype(jnp.bfloat16), axis)
    place = jnp.arange(count, dtype=jnp.int32)
    if backward:
        between = (place[None, :] < place[:, None]) & (place[None, :] > mine)
        used = place > mine
    else:
        between = (place[None, :] > place[:, None]) & (place[None, :] < mine)
        used = place < mine
    decay = jnp.sum(
        jnp.where(between[:, :, None, None], log_totals[None], 0.0), axis=1
    )
    weight = jnp.where(used[:, None, None], jnp.exp(decay), 0.0)
    return jnp.sum(weight[..., None, None] * pieces.astype(jnp.float32), axis=0)


def summed_share(value, axis):
    count = lax.axis_size(axis)
    pieces = value.astype(jnp.bfloat16).reshape(count, value.shape[0] // count, *value.shape[1:])
    landed = lax.all_to_all(pieces, axis, 0, 0)
    return jnp.sum(landed.astype(jnp.float32), axis=0)


def summed_rows(value, axis):
    count = lax.axis_size(axis)
    sequences, rows, width = value.shape
    pieces = value.astype(jnp.bfloat16).reshape(sequences, count, rows // count, width)
    landed = lax.all_to_all(pieces, axis, 1, 1)
    return jnp.sum(landed.astype(jnp.float32), axis=1)


def summed_everywhere(value, axis):
    share = summed_share(value, axis).astype(jnp.bfloat16)
    return lax.all_gather(share, axis, axis=0, tiled=True).astype(jnp.float32)


def matmul(left_operand, right_operand):
    return jnp.einsum(
        "std,de->ste", left_operand, right_operand, preferred_element_type=jnp.float32
    )


def matmul_back(grad, right_operand):
    return jnp.einsum("ste,de->std", grad, right_operand, preferred_element_type=jnp.float32)


def weight_grad(left_operand, grad):
    return jnp.einsum("std,ste->de", left_operand, grad, preferred_element_type=jnp.float32)


def rms_norm(values, gain):
    factor = lax.rsqrt(jnp.mean(values * values, axis=-1, keepdims=True) + EPSILON)
    return values * factor * gain


def rotate(values, positions):
    half = values.shape[-1] // 2
    freq = ROPE_BASE ** (-jnp.arange(half, dtype=jnp.float32) * 2.0 / values.shape[-1])
    angle = positions[:, None] * freq[None, :]
    cosine = jnp.cos(angle)[None, :, None, :]
    sine = jnp.sin(angle)[None, :, None, :]
    first = values[..., :half]
    second = values[..., half:]
    return jnp.concatenate(
        [first * cosine - second * sine, second * cosine + first * sine], axis=-1
    )


def block_scores(queries, keys, query_pos, key_pos, factor):
    scores = (
        jnp.einsum("sqhd,skd->shqk", queries, keys, preferred_element_type=jnp.float32) * factor
    )
    allowed = key_pos[None, :] <= query_pos[:, None]
    return jnp.where(allowed[None, None], scores, MASKED)


def conv_act(extended, conv_weight):
    rows = extended.shape[1] - (conv_weight.shape[0] - 1)
    summed = extended[:, 0:rows] * conv_weight[0]
    for tap in range(1, conv_weight.shape[0]):
        summed = summed + extended[:, tap : tap + rows] * conv_weight[tap]
    return jax.nn.silu(summed)


def ssm_inputs(extended, step_raw, conv_weight, step_bias, decay_log):
    activated = conv_act(extended, conv_weight)
    inner_width = activated.shape[-1] - 2 * STATE
    heads_here = step_raw.shape[-1]
    channels = activated[..., :inner_width].reshape(
        activated.shape[0], activated.shape[1], heads_here, inner_width // heads_here
    )
    writes = activated[..., inner_width : inner_width + STATE]
    reads = activated[..., inner_width + STATE :]
    step = jax.nn.softplus(step_raw + step_bias)
    logdecay = -step * jnp.exp(decay_log)
    return (channels, writes, reads, step, logdecay)


def intra(channels, writes, reads, step, running):
    rows = running.shape[1]
    lower = jnp.arange(rows, dtype=jnp.int32)[:, None] >= jnp.arange(rows, dtype=jnp.int32)[None, :]
    mask = lower[None, :, :, None]
    spread = running[:, :, None, :] - running[:, None, :, :]
    decay = jnp.where(mask, jnp.exp(jnp.where(mask, spread, 0.0)), 0.0)
    intersection = jnp.einsum("stn,sun->stu", reads, writes, precision=HIGH_ACCURACY)
    mixing = decay * intersection[..., None] * step[:, None, :, :]
    within = jnp.einsum("stuh,suhp->sthp", mixing, channels, precision=HIGH_ACCURACY)
    tail_weight = jnp.exp(running[:, -1:, :] - running) * step
    local = jnp.einsum("suh,suhp,sun->shpn", tail_weight, channels, writes, precision=HIGH_ACCURACY)
    return (within, local)


def inter(reads, running, state):
    return jnp.exp(running)[..., None] * jnp.einsum(
        "stn,shpn->sthp", reads, state, precision=HIGH_ACCURACY
    )


def ssm_full(extended, step_raw, conv_weight, step_bias, decay_log, skip_gain, state_in):
    channels, writes, reads, step, logdecay = ssm_inputs(
        extended, step_raw, conv_weight, step_bias, decay_log
    )
    running = running_sum(logdecay)
    within, local = intra(channels, writes, reads, step, running)
    result = within + inter(reads, running, state_in) + skip_gain[:, None] * channels
    state_end = jnp.exp(running[:, -1])[:, :, None, None] * state_in + local
    return (result, state_end)


def running_sum(values):
    rows = values.shape[1]
    lower = jnp.arange(rows, dtype=jnp.int32)[:, None] >= jnp.arange(rows, dtype=jnp.int32)[None, :]
    return jnp.einsum(
        "tu,suh->sth", lower.astype(jnp.float32), values, precision=HIGH_ACCURACY
    )


def on_device(
    hidden_in,
    norm_gain,
    query_weight,
    keyvalue_matrix,
    output_weight,
    zgate_weight,
    inner_weight,
    state_weight,
    step_weight,
    conv_inner,
    conv_state,
    step_bias,
    decay_log,
    skip_gain,
    ssm_gain,
    mixer_weight,
    mlp_gain,
    gate_weight,
    up_weight,
    down_weight,
    grad_output,
):
    sequences, rows, width = hidden_in.shape
    head_dim = keyvalue_matrix.shape[2] // 2
    heads_here = query_weight.shape[1] // head_dim
    group = HEADS // KV_HEADS
    factor = head_dim ** (-0.5)
    inner_width = inner_weight.shape[1]
    mamba_here = step_bias.shape[0]
    seq_index = lax.axis_index("seq")
    head_index = lax.axis_index("head")
    query_pos = seq_index * rows + jnp.arange(rows, dtype=jnp.int32)
    positions = query_pos.astype(jnp.float32)
    input_float = hidden_in.astype(jnp.float32)
    gain_one = norm_gain.astype(jnp.float32)
    normalized_input = rms_norm(input_float, gain_one).astype(jnp.bfloat16)
    query_raw = matmul(normalized_input, query_weight).reshape(
        sequences, rows, heads_here, head_dim
    )
    queries = rotate(query_raw, positions).astype(jnp.bfloat16)
    kv_index = head_index * heads_here // group
    own_weight = lax.dynamic_index_in_dim(keyvalue_matrix, kv_index, 1, keepdims=False)
    keyvalue_projected = matmul(normalized_input, own_weight)
    keys_own = rotate(keyvalue_projected[:, :, None, :head_dim], positions)[:, :, 0]
    keyvalue_own = jnp.concatenate([keys_own, keyvalue_projected[..., head_dim:]], axis=-1).astype(
        jnp.bfloat16
    )
    keyvalue_all = lax.all_gather(keyvalue_own, "seq", axis=1, tiled=True)
    length = keyvalue_all.shape[1]
    key_block = math.gcd(length, 512)
    blocks_needed = ((seq_index + 1) * rows + key_block - 1) // key_block

    def key_piece(index):
        start = index * key_block
        piece = lax.dynamic_slice_in_dim(keyvalue_all, start, key_block, 1)
        return (
            piece[..., :head_dim],
            piece[..., head_dim:],
            start + jnp.arange(key_block, dtype=jnp.int32),
        )

    def first_pass(index, carry):
        peak, total = carry
        keys, values, key_pos = key_piece(index)
        scores = block_scores(queries, keys, query_pos, key_pos, factor)
        new_peak = jnp.maximum(peak, jnp.max(scores, axis=-1))
        total = total * jnp.exp(peak - new_peak) + jnp.sum(
            jnp.exp(scores - new_peak[..., None]), axis=-1
        )
        return (new_peak, total)

    start_peak = jnp.full((sequences, heads_here, rows), MASKED, jnp.float32)
    peak, total = lax.fori_loop(
        0, blocks_needed, first_pass, (start_peak, jnp.zeros_like(start_peak))
    )
    log_total = peak + jnp.log(total)

    def second_pass(index, summed):
        keys, values, key_pos = key_piece(index)
        scores = block_scores(queries, keys, query_pos, key_pos, factor)
        probs = jnp.exp(scores - log_total[..., None]).astype(jnp.bfloat16)
        return summed + jnp.einsum(
            "shqk,skd->sqhd", probs, values, preferred_element_type=jnp.float32
        )

    attended_float = lax.fori_loop(
        0,
        blocks_needed,
        second_pass,
        jnp.zeros((sequences, rows, heads_here, head_dim), jnp.float32),
    )
    attended = attended_float.astype(jnp.bfloat16).reshape(sequences, rows, heads_here * head_dim)
    zgate = matmul(normalized_input, zgate_weight)
    inner = jnp.concatenate(
        [matmul(normalized_input, inner_weight), matmul(normalized_input, state_weight)], axis=-1
    )
    step_raw = matmul(normalized_input, step_weight)
    conv_weight = jnp.concatenate([conv_inner, conv_state], axis=1).astype(jnp.float32)
    taps = conv_weight.shape[0]
    before = passed_along(inner[:, rows - (taps - 1) :], "seq", 1)
    extended = jnp.concatenate([before, inner], axis=1)
    channels, writes, reads, step, logdecay = ssm_inputs(
        extended, step_raw, conv_weight, step_bias, decay_log
    )
    running = running_sum(logdecay)
    within, local = intra(channels, writes, reads, step, running)
    log_totals = lax.all_gather(running[:, -1], "seq")
    state_in = carried(log_totals, local, "seq", False)
    y_ssm = within + inter(reads, running, state_in) + skip_gain[:, None] * channels
    y_flat = y_ssm.reshape(sequences, rows, inner_width)
    gated = y_flat * jax.nn.silu(zgate)
    squares = lax.psum(jnp.sum(gated * gated, axis=-1), "head")
    ssm_factor = lax.rsqrt(squares / SSM + EPSILON)[..., None]
    gain_ssm = ssm_gain.astype(jnp.float32)
    ssm_normed = (gated * ssm_factor * gain_ssm).astype(jnp.bfloat16)
    branch_part = matmul(attended, output_weight) + matmul(ssm_normed, mixer_weight)
    quarter = rows // lax.axis_size("head")
    mixed_rows = summed_rows(branch_part, "head")
    def own_rows(value):
        return lax.dynamic_slice_in_dim(value, head_index * quarter, quarter, 1)

    input_rows = own_rows(input_float)
    hidden_rows = input_rows + mixed_rows
    gain_two = mlp_gain.astype(jnp.float32)
    normed_two_rows = rms_norm(hidden_rows, gain_two).astype(jnp.bfloat16)
    normed_two = lax.all_gather(normed_two_rows, "head", axis=1, tiled=True)
    gate = matmul(normed_two, gate_weight)
    up = matmul(normed_two, up_weight)
    activated = (jax.nn.silu(gate) * up).astype(jnp.bfloat16)
    feed_part = matmul(activated, down_weight)
    feed_own = summed_rows(feed_part, "head")
    output_own = (hidden_rows + feed_own).astype(jnp.bfloat16)
    output = lax.all_gather(output_own, "head", axis=1, tiled=True)
    act_grad = matmul_back(grad_output, down_weight)
    grad_down = weight_grad(activated, grad_output)
    gate_pull = jax.vjp(lambda gate_in, up_in: jax.nn.silu(gate_in) * up_in, gate, up)[1]
    gate_grad, up_grad = gate_pull(act_grad)
    gate_grad = gate_grad.astype(jnp.bfloat16)
    up_grad = up_grad.astype(jnp.bfloat16)
    grad_gate = weight_grad(normed_two, gate_grad)
    grad_up = weight_grad(normed_two, up_grad)
    normed_two_grad = summed_rows(
        matmul_back(gate_grad, gate_weight) + matmul_back(up_grad, up_weight), "head"
    )
    units = grad_down.shape[0]
    down_sum = summed_everywhere(grad_down, "seq")
    feed_sums = summed_everywhere(jnp.concatenate([grad_gate, grad_up], axis=1), "seq")
    norm_two_pull = jax.vjp(rms_norm, hidden_rows, gain_two)[1]
    hidden_norm_grad, grad_gain_two = norm_two_pull(normed_two_grad)
    hidden_grad = own_rows(grad_output).astype(jnp.float32) + hidden_norm_grad
    mixed_grad = lax.all_gather(
        hidden_grad.astype(jnp.bfloat16), "head", axis=1, tiled=True
    )
    grad_output_proj = weight_grad(attended, mixed_grad)
    attended_grad = (
        matmul_back(mixed_grad, output_weight)
        .astype(jnp.bfloat16)
        .reshape(sequences, rows, heads_here, head_dim)
    )
    grad_mixer = weight_grad(ssm_normed, mixed_grad)
    mixed_sums = summed_everywhere(jnp.concatenate([grad_output_proj, grad_mixer], axis=0), "seq")
    ssm_normed_grad = matmul_back(mixed_grad, mixer_weight)
    weighted = ssm_normed_grad * gain_ssm
    inner_total = lax.psum(jnp.sum(weighted * gated, axis=-1), "head")
    gated_grad = weighted * ssm_factor - gated * ssm_factor**3 * inner_total[..., None] / SSM
    grad_gain_ssm = jnp.sum(ssm_normed_grad * gated * ssm_factor, axis=(0, 1))
    gated_pull = jax.vjp(lambda y_in, z_in: y_in * jax.nn.silu(z_in), y_flat, zgate)[1]
    y_grad, zgate_grad = gated_pull(gated_grad)
    zgate_grad = zgate_grad.astype(jnp.bfloat16)
    grad_zgate = weight_grad(normalized_input, zgate_grad)
    y_grad_heads = y_grad.reshape(sequences, rows, mamba_here, inner_width // mamba_here)
    own_state_grad = jnp.einsum(
        "sth,stn,sthp->shpn", jnp.exp(running), reads, y_grad_heads, precision=HIGH_ACCURACY
    )
    state_grad = carried(log_totals, own_state_grad, "seq", True)
    ssm_pull = jax.vjp(
        ssm_full, extended, step_raw, conv_weight, step_bias, decay_log, skip_gain, state_in
    )[1]
    extended_grad, step_raw_grad, conv_grad, grad_step_bias, grad_decay_log, grad_skip, unused = (
        ssm_pull((y_grad_heads, state_grad))
    )
    before_grad = passed_along(extended_grad[:, : taps - 1], "seq", -1)
    inner_grad = extended_grad[:, taps - 1 :] + jnp.pad(
        before_grad, ((0, 0), (rows - (taps - 1), 0), (0, 0))
    )
    inner_own = inner_grad[..., :inner_width].astype(jnp.bfloat16)
    step_grad = step_raw_grad.astype(jnp.bfloat16)
    grad_inner = weight_grad(normalized_input, inner_own)
    grad_step = weight_grad(normalized_input, step_grad)
    delta = jnp.sum(attended_grad.astype(jnp.float32) * attended_float, axis=-1).transpose(0, 2, 1)

    def make_back_pass():

        def back_pass(index, carry):
            query_grad, keyvalue_grad = carry
            keys, values, key_pos = key_piece(index)
            scores = block_scores(queries, keys, query_pos, key_pos, factor)
            probs = jnp.exp(scores - log_total[..., None])
            probs_grad = jnp.einsum(
                "sqhd,skd->shqk", attended_grad, values, preferred_element_type=jnp.float32
            )
            scores_grad = (probs * (probs_grad - delta[..., None])).astype(jnp.bfloat16)
            query_grad = (
                query_grad
                + jnp.einsum(
                    "shqk,skd->sqhd", scores_grad, keys, preferred_element_type=jnp.float32
                )
                * factor
            )
            key_grad = (
                jnp.einsum(
                    "shqk,sqhd->skd", scores_grad, queries, preferred_element_type=jnp.float32
                )
                * factor
            )
            value_grad = jnp.einsum(
                "shqk,sqhd->skd",
                probs.astype(jnp.bfloat16),
                attended_grad,
                preferred_element_type=jnp.float32,
            )
            keyvalue_grad = lax.dynamic_update_slice_in_dim(
                keyvalue_grad,
                jnp.concatenate([key_grad, value_grad], axis=-1),
                index * key_block,
                1,
            )
            return (query_grad, keyvalue_grad)

        return back_pass

    query_zero = jnp.zeros((sequences, rows, heads_here, head_dim), jnp.float32)
    keyvalue_zero = jnp.zeros((sequences, length, 2 * head_dim), jnp.float32)
    query_grad, keyvalue_grad_all = lax.fori_loop(
        0, blocks_needed, make_back_pass(), (query_zero, keyvalue_zero)
    )
    keyvalue_grad_own = summed_rows(keyvalue_grad_all, "seq")
    key_raw_grad = rotate(keyvalue_grad_own[:, :, None, :head_dim], -positions)[:, :, 0]
    keyvalue_raw_grad = jnp.concatenate([key_raw_grad, keyvalue_grad_own[..., head_dim:]], axis=-1)
    chooser = (jnp.arange(KV_HEADS, dtype=jnp.int32) == kv_index).astype(jnp.float32)
    keyvalue_both = chooser[None, None, :, None] * keyvalue_raw_grad[:, :, None, :]
    query_raw_grad = (
        rotate(query_grad, -positions)
        .astype(jnp.bfloat16)
        .reshape(sequences, rows, heads_here * head_dim)
    )
    grad_query = weight_grad(normalized_input, query_raw_grad)
    normed_part = (
        matmul_back(query_raw_grad, query_weight)
        + matmul_back(zgate_grad, zgate_weight)
        + matmul_back(inner_own, inner_weight)
        + matmul_back(step_grad, step_weight)
    )
    kv_width = keyvalue_both.shape[2] * keyvalue_both.shape[3]
    together = summed_rows(
        jnp.concatenate(
            [
                normed_part,
                keyvalue_both.reshape(sequences, rows, kv_width),
                inner_grad[..., inner_width:],
            ],
            axis=-1,
        ),
        "head",
    )
    normed_sum = together[..., :width]
    low_rows = together[..., width:].astype(jnp.bfloat16)
    shared_weight = jnp.concatenate(
        [keyvalue_matrix.reshape(width, kv_width), state_weight], axis=1
    )
    grad_shared = weight_grad(own_rows(normalized_input), low_rows)
    normed_grad = normed_sum + matmul_back(low_rows, shared_weight)
    norm_one_pull = jax.vjp(rms_norm, input_rows, gain_one)[1]
    input_norm_grad, grad_gain_one = norm_one_pull(normed_grad)
    input_rows_grad = (hidden_grad + input_norm_grad).astype(jnp.bfloat16)
    grad_input = lax.all_gather(input_rows_grad, "head", axis=1, tiled=True).astype(jnp.float32)
    last_sums = summed_everywhere(
        jnp.concatenate([grad_zgate, grad_inner, grad_query], axis=1), "seq"
    )
    shared_part = summed_share(summed_share(grad_shared, "head"), "seq").astype(jnp.bfloat16)
    shared_sum = lax.all_gather(
        shared_part, ("head", "seq"), axis=0, tiled=True
    ).astype(jnp.float32)
    own_small = [
        grad_step,
        conv_grad[:, :inner_width],
        grad_step_bias,
        grad_decay_log,
        grad_skip,
        grad_gain_ssm,
    ]
    all_small = [grad_gain_one, grad_gain_two, conv_grad[:, inner_width:]]

    def unpacked(flat, likes):
        found, at = [], 0
        for like in likes:
            found.append(flat[at : at + like.size].reshape(like.shape))
            at += like.size
        return found

    own_flat = lax.psum(jnp.concatenate([part.reshape(-1) for part in own_small]), "seq")
    all_flat = lax.psum(
        jnp.concatenate([part.reshape(-1) for part in all_small]), ("seq", "head")
    )
    grad_step, conv_inner_grad, grad_step_bias, grad_decay_log, grad_skip, grad_gain_ssm = unpacked(
        own_flat, own_small
    )
    grad_gain_one, grad_gain_two, conv_state_grad = unpacked(all_flat, all_small)
    attended_width = heads_here * head_dim
    return (
        output,
        grad_input,
        grad_gain_one,
        last_sums[:, 2 * inner_width :],
        shared_sum[:, :kv_width].reshape(keyvalue_matrix.shape),
        mixed_sums[:attended_width],
        last_sums[:, :inner_width],
        last_sums[:, inner_width : 2 * inner_width],
        shared_sum[:, kv_width:],
        grad_step,
        conv_inner_grad,
        conv_state_grad,
        grad_step_bias,
        grad_decay_log,
        grad_skip,
        grad_gain_ssm,
        mixed_sums[attended_width:],
        grad_gain_two,
        feed_sums[:, :units],
        feed_sums[:, units:],
        down_sum,
    )


def solution(mesh):
    placed = (
        P(None, "seq", None),
        P(),
        P(None, "head"),
        P(),
        P("head", None),
        P(None, "head"),
        P(None, "head"),
        P(),
        P(None, "head"),
        P(None, "head"),
        P(),
        P("head"),
        P("head"),
        P("head"),
        P("head"),
        P("head", None),
        P(),
        P(None, "head"),
        P(None, "head"),
        P("head", None),
        P(None, "seq", None),
    )
    return jax.shard_map(
        on_device,
        mesh=mesh,
        in_specs=placed,
        out_specs=(
            P(None, "seq", None),
            P(None, "seq", None),
            P(),
            P(None, "head"),
            P(),
            P("head", None),
            P(None, "head"),
            P(None, "head"),
            P(),
            P(None, "head"),
            P(None, "head"),
            P(),
            P("head"),
            P("head"),
            P("head"),
            P("head"),
            P("head", None),
            P(),
            P(None, "head"),
            P(None, "head"),
            P("head", None),
        ),
        check_vma=False,
    )
```

```python
import math

import jax
import jax.numpy as jnp
from jax import lax
from jax.sharding import PartitionSpec as P

HEADS = 8
KV_HEADS = 2
STATE = 128
SSM = 1536


HIGH_ACCURACY = lax.Precision.HIGHEST
EPSILON = 1e-05
ROPE_BASE = 100000000000.0
MASKED = -1e30


def passed_along(value, axis, steps):
    count = lax.axis_size(axis)
    first, last = (max(0, -steps), min(count, count - steps))
    return lax.ppermute(value, axis, [(source, source + steps) for source in range(first, last)])


def carried(log_totals, states, axis, backward):
    count, mine = (lax.axis_size(axis), lax.axis_index(axis))
    pieces = lax.all_gather(states.astype(jnp.bfloat16), axis)
    place = jnp.arange(count, dtype=jnp.int32)
    if backward:
        between = (place[None, :] < place[:, None]) & (place[None, :] > mine)
        used = place > mine
    else:
        between = (place[None, :] > place[:, None]) & (place[None, :] < mine)
        used = place < mine
    decay = jnp.sum(
        jnp.where(between[:, :, None, None], log_totals[None], 0.0), axis=1
    )
    weight = jnp.where(used[:, None, None], jnp.exp(decay), 0.0)
    return jnp.sum(weight[..., None, None] * pieces.astype(jnp.float32), axis=0)


def summed_share(value, axis):
    count = lax.axis_size(axis)
    pieces = value.astype(jnp.bfloat16).reshape(count, value.shape[0] // count, *value.shape[1:])
    landed = lax.all_to_all(pieces, axis, 0, 0)
    return jnp.sum(landed.astype(jnp.float32), axis=0)


def summed_rows(value, axis):
    count = lax.axis_size(axis)
    sequences, rows, width = value.shape
    pieces = value.astype(jnp.bfloat16).reshape(sequences, count, rows // count, width)
    landed = lax.all_to_all(pieces, axis, 1, 1)
    return jnp.sum(landed.astype(jnp.float32), axis=1)


def two_parts(values, rows):
    flat = jnp.concatenate([part.reshape(-1) for part in values])
    flat = jnp.pad(flat, (0, -flat.size % rows)).reshape(rows, -1)
    high = lax.reduce_precision(flat, 8, 7)
    return jnp.concatenate([high, flat - high], axis=1)


def joined(columns, likes):
    half = columns.shape[1] // 2
    flat = (columns[:, :half] + columns[:, half:]).reshape(-1)
    found, at = [], 0
    for like in likes:
        found.append(flat[at : at + like.size].reshape(like.shape))
        at += like.size
    return found


def split_again(share, plain):
    half = (share.shape[1] - plain) // 2
    flat = share[:, plain : plain + half] + share[:, plain + half :]
    high = lax.reduce_precision(flat, 8, 7)
    return jnp.concatenate([share[:, :plain], high, flat - high], axis=1).astype(jnp.bfloat16)


def summed_everywhere(value, axis):
    share = lax.psum_scatter(
        value.astype(jnp.bfloat16), axis, scatter_dimension=0, tiled=True
    )
    return lax.all_gather(share, axis, axis=0, tiled=True).astype(jnp.float32)


def matmul(left_operand, right_operand):
    return jnp.einsum(
        "std,de->ste", left_operand, right_operand, preferred_element_type=jnp.float32
    )


def matmul_back(grad, right_operand):
    return jnp.einsum("ste,de->std", grad, right_operand, preferred_element_type=jnp.float32)


def weight_grad(left_operand, grad):
    return jnp.einsum("std,ste->de", left_operand, grad, preferred_element_type=jnp.float32)


def rms_norm(values, gain):
    factor = lax.rsqrt(jnp.mean(values * values, axis=-1, keepdims=True) + EPSILON)
    return values * factor * gain


def rotate(values, positions):
    half = values.shape[-1] // 2
    freq = ROPE_BASE ** (-jnp.arange(half, dtype=jnp.float32) * 2.0 / values.shape[-1])
    angle = positions[:, None] * freq[None, :]
    cosine = jnp.cos(angle)[None, :, None, :]
    sine = jnp.sin(angle)[None, :, None, :]
    first = values[..., :half]
    second = values[..., half:]
    return jnp.concatenate(
        [first * cosine - second * sine, second * cosine + first * sine], axis=-1
    )


def block_scores(queries, keys, query_pos, key_pos, factor):
    scores = (
        jnp.einsum("sqhd,skd->shqk", queries, keys, preferred_element_type=jnp.float32) * factor
    )
    allowed = key_pos[None, :] <= query_pos[:, None]
    return jnp.where(allowed[None, None], scores, MASKED)


def conv_act(extended, conv_weight):
    rows = extended.shape[1] - (conv_weight.shape[0] - 1)
    summed = extended[:, 0:rows] * conv_weight[0]
    for tap in range(1, conv_weight.shape[0]):
        summed = summed + extended[:, tap : tap + rows] * conv_weight[tap]
    return jax.nn.silu(summed)


def ssm_inputs(extended, step_raw, conv_weight, step_bias, decay_log):
    activated = conv_act(extended, conv_weight)
    inner_width = activated.shape[-1] - 2 * STATE
    heads_here = step_raw.shape[-1]
    channels = activated[..., :inner_width].reshape(
        activated.shape[0], activated.shape[1], heads_here, inner_width // heads_here
    )
    writes = activated[..., inner_width : inner_width + STATE]
    reads = activated[..., inner_width + STATE :]
    step = jax.nn.softplus(step_raw + step_bias)
    logdecay = -step * jnp.exp(decay_log)
    return (channels, writes, reads, step, logdecay)


def intra(channels, writes, reads, step, running):
    rows = running.shape[1]
    lower = jnp.arange(rows, dtype=jnp.int32)[:, None] >= jnp.arange(rows, dtype=jnp.int32)[None, :]
    mask = lower[None, :, :, None]
    spread = running[:, :, None, :] - running[:, None, :, :]
    decay = jnp.where(mask, jnp.exp(jnp.where(mask, spread, 0.0)), 0.0)
    intersection = jnp.einsum("stn,sun->stu", reads, writes, precision=HIGH_ACCURACY)
    mixing = decay * intersection[..., None] * step[:, None, :, :]
    within = jnp.einsum("stuh,suhp->sthp", mixing, channels, precision=HIGH_ACCURACY)
    tail_weight = jnp.exp(running[:, -1:, :] - running) * step
    local = jnp.einsum("suh,suhp,sun->shpn", tail_weight, channels, writes, precision=HIGH_ACCURACY)
    return (within, local)


def inter(reads, running, state):
    return jnp.exp(running)[..., None] * jnp.einsum(
        "stn,shpn->sthp", reads, state, precision=HIGH_ACCURACY
    )


def ssm_full(extended, step_raw, conv_weight, step_bias, decay_log, skip_gain, state_in):
    channels, writes, reads, step, logdecay = ssm_inputs(
        extended, step_raw, conv_weight, step_bias, decay_log
    )
    running = running_sum(logdecay)
    within, local = intra(channels, writes, reads, step, running)
    result = within + inter(reads, running, state_in) + skip_gain[:, None] * channels
    state_end = jnp.exp(running[:, -1])[:, :, None, None] * state_in + local
    return (result, state_end)


def running_sum(values):
    rows = values.shape[1]
    lower = jnp.arange(rows, dtype=jnp.int32)[:, None] >= jnp.arange(rows, dtype=jnp.int32)[None, :]
    return jnp.einsum(
        "tu,suh->sth", lower.astype(jnp.float32), values, precision=HIGH_ACCURACY
    )


def on_device(
    hidden_in,
    norm_gain,
    query_weight,
    keyvalue_matrix,
    output_weight,
    zgate_weight,
    inner_weight,
    state_weight,
    step_weight,
    conv_inner,
    conv_state,
    step_bias,
    decay_log,
    skip_gain,
    ssm_gain,
    mixer_weight,
    mlp_gain,
    gate_weight,
    up_weight,
    down_weight,
    grad_output,
):
    sequences, rows, width = hidden_in.shape
    head_dim = keyvalue_matrix.shape[2] // 2
    heads_here = query_weight.shape[1] // head_dim
    group = HEADS // KV_HEADS
    factor = head_dim ** (-0.5)
    inner_width = inner_weight.shape[1]
    mamba_here = step_bias.shape[0]
    seq_index = lax.axis_index("seq")
    head_index = lax.axis_index("head")
    query_pos = seq_index * rows + jnp.arange(rows, dtype=jnp.int32)
    positions = query_pos.astype(jnp.float32)
    input_float = hidden_in.astype(jnp.float32)
    gain_one = norm_gain.astype(jnp.float32)
    normalized_input = rms_norm(input_float, gain_one).astype(jnp.bfloat16)
    query_raw = matmul(normalized_input, query_weight).reshape(
        sequences, rows, heads_here, head_dim
    )
    queries = rotate(query_raw, positions).astype(jnp.bfloat16)
    kv_index = head_index * heads_here // group
    own_weight = lax.dynamic_index_in_dim(keyvalue_matrix, kv_index, 1, keepdims=False)
    keyvalue_projected = matmul(normalized_input, own_weight)
    keys_own = rotate(keyvalue_projected[:, :, None, :head_dim], positions)[:, :, 0]
    keyvalue_own = jnp.concatenate([keys_own, keyvalue_projected[..., head_dim:]], axis=-1).astype(
        jnp.bfloat16
    )
    keyvalue_all = lax.all_gather(keyvalue_own, "seq", axis=1, tiled=True)
    length = keyvalue_all.shape[1]
    key_block = math.gcd(length, 512)
    blocks_needed = ((seq_index + 1) * rows + key_block - 1) // key_block

    def key_piece(index):
        start = index * key_block
        piece = lax.dynamic_slice_in_dim(keyvalue_all, start, key_block, 1)
        return (
            piece[..., :head_dim],
            piece[..., head_dim:],
            start + jnp.arange(key_block, dtype=jnp.int32),
        )

    def forward_pass(index, carry):
        peak, total, summed = carry
        keys, values, key_pos = key_piece(index)
        scores = block_scores(queries, keys, query_pos, key_pos, factor)
        new_peak = jnp.maximum(peak, jnp.max(scores, axis=-1))
        kept = jnp.exp(peak - new_peak)
        terms = jnp.exp(scores - new_peak[..., None])
        total = total * kept + jnp.sum(terms, axis=-1)
        summed = summed * kept[..., None] + jnp.einsum(
            "shqk,skd->shqd",
            terms.astype(jnp.bfloat16),
            values,
            preferred_element_type=jnp.float32,
        )
        return (new_peak, total, summed)

    start_peak = jnp.full((sequences, heads_here, rows), MASKED, jnp.float32)
    peak, total, summed = lax.fori_loop(
        0,
        blocks_needed,
        forward_pass,
        (
            start_peak,
            jnp.zeros_like(start_peak),
            jnp.zeros((sequences, heads_here, rows, head_dim), jnp.float32),
        ),
    )
    log_total = peak + jnp.log(total)
    attended_float = (summed / total[..., None]).transpose(0, 2, 1, 3)
    attended = attended_float.astype(jnp.bfloat16).reshape(sequences, rows, heads_here * head_dim)
    zgate = matmul(normalized_input, zgate_weight)
    inner = jnp.concatenate(
        [matmul(normalized_input, inner_weight), matmul(normalized_input, state_weight)], axis=-1
    )
    step_raw = matmul(normalized_input, step_weight)
    conv_weight = jnp.concatenate([conv_inner, conv_state], axis=1).astype(jnp.float32)
    taps = conv_weight.shape[0]
    before = passed_along(inner[:, rows - (taps - 1) :], "seq", 1)
    extended = jnp.concatenate([before, inner], axis=1)
    channels, writes, reads, step, logdecay = ssm_inputs(
        extended, step_raw, conv_weight, step_bias, decay_log
    )
    running = running_sum(logdecay)
    within, local = intra(channels, writes, reads, step, running)
    log_totals = lax.all_gather(running[:, -1], "seq")
    state_in = carried(log_totals, local, "seq", False)
    y_ssm = within + inter(reads, running, state_in) + skip_gain[:, None] * channels
    y_flat = y_ssm.reshape(sequences, rows, inner_width)
    gated = y_flat * jax.nn.silu(zgate)
    squares = lax.psum(jnp.sum(gated * gated, axis=-1), "head")
    ssm_factor = lax.rsqrt(squares / SSM + EPSILON)[..., None]
    gain_ssm = ssm_gain.astype(jnp.float32)
    ssm_normed = (gated * ssm_factor * gain_ssm).astype(jnp.bfloat16)
    branch_part = matmul(attended, output_weight) + matmul(ssm_normed, mixer_weight)
    quarter = rows // lax.axis_size("head")
    mixed_rows = summed_rows(branch_part, "head")
    def own_rows(value):
        return lax.dynamic_slice_in_dim(value, head_index * quarter, quarter, 1)

    input_rows = own_rows(input_float)
    hidden_rows = input_rows + mixed_rows
    gain_two = mlp_gain.astype(jnp.float32)
    normed_two_rows = rms_norm(hidden_rows, gain_two).astype(jnp.bfloat16)
    normed_two = lax.all_gather(normed_two_rows, "head", axis=1, tiled=True)
    gate = matmul(normed_two, gate_weight)
    up = matmul(normed_two, up_weight)
    activated = (jax.nn.silu(gate) * up).astype(jnp.bfloat16)
    feed_part = matmul(activated, down_weight)
    feed_own = lax.psum_scatter(
        feed_part.astype(jnp.bfloat16), "head", scatter_dimension=1, tiled=True
    ).astype(jnp.float32)
    output_own = (hidden_rows + feed_own).astype(jnp.bfloat16)
    output = lax.all_gather(output_own, "head", axis=1, tiled=True)
    act_grad = matmul_back(grad_output, down_weight)
    grad_down = weight_grad(activated, grad_output)
    gate_pull = jax.vjp(lambda gate_in, up_in: jax.nn.silu(gate_in) * up_in, gate, up)[1]
    gate_grad, up_grad = gate_pull(act_grad)
    gate_grad = gate_grad.astype(jnp.bfloat16)
    up_grad = up_grad.astype(jnp.bfloat16)
    grad_gate = weight_grad(normed_two, gate_grad)
    grad_up = weight_grad(normed_two, up_grad)
    normed_two_grad = summed_rows(
        matmul_back(gate_grad, gate_weight) + matmul_back(up_grad, up_weight), "head"
    )
    units = grad_down.shape[0]
    down_sum = summed_everywhere(grad_down, "seq")
    feed_sums = summed_everywhere(jnp.concatenate([grad_gate, grad_up], axis=1), "seq")
    norm_two_pull = jax.vjp(rms_norm, hidden_rows, gain_two)[1]
    hidden_norm_grad, grad_gain_two = norm_two_pull(normed_two_grad)
    hidden_grad = own_rows(grad_output).astype(jnp.float32) + hidden_norm_grad
    mixed_grad = lax.all_gather(
        hidden_grad.astype(jnp.bfloat16), "head", axis=1, tiled=True
    )
    grad_output_proj = weight_grad(attended, mixed_grad)
    attended_grad = (
        matmul_back(mixed_grad, output_weight)
        .astype(jnp.bfloat16)
        .reshape(sequences, rows, heads_here, head_dim)
    )
    grad_mixer = weight_grad(ssm_normed, mixed_grad)
    mixed_sums = summed_everywhere(jnp.concatenate([grad_output_proj, grad_mixer], axis=0), "seq")
    ssm_normed_grad = matmul_back(mixed_grad, mixer_weight)
    weighted = ssm_normed_grad * gain_ssm
    inner_total = lax.psum(jnp.sum(weighted * gated, axis=-1), "head")
    gated_grad = weighted * ssm_factor - gated * ssm_factor**3 * inner_total[..., None] / SSM
    grad_gain_ssm = jnp.sum(ssm_normed_grad * gated * ssm_factor, axis=(0, 1))
    gated_pull = jax.vjp(lambda y_in, z_in: y_in * jax.nn.silu(z_in), y_flat, zgate)[1]
    y_grad, zgate_grad = gated_pull(gated_grad)
    zgate_grad = zgate_grad.astype(jnp.bfloat16)
    grad_zgate = weight_grad(normalized_input, zgate_grad)
    y_grad_heads = y_grad.reshape(sequences, rows, mamba_here, inner_width // mamba_here)
    own_state_grad = jnp.einsum(
        "sth,stn,sthp->shpn", jnp.exp(running), reads, y_grad_heads, precision=HIGH_ACCURACY
    )
    state_grad = carried(log_totals, own_state_grad, "seq", True)
    ssm_pull = jax.vjp(
        ssm_full, extended, step_raw, conv_weight, step_bias, decay_log, skip_gain, state_in
    )[1]
    extended_grad, step_raw_grad, conv_grad, grad_step_bias, grad_decay_log, grad_skip, unused = (
        ssm_pull((y_grad_heads, state_grad))
    )
    before_grad = passed_along(extended_grad[:, : taps - 1], "seq", -1)
    inner_grad = extended_grad[:, taps - 1 :] + jnp.pad(
        before_grad, ((0, 0), (rows - (taps - 1), 0), (0, 0))
    )
    inner_own = inner_grad[..., :inner_width].astype(jnp.bfloat16)
    step_grad = step_raw_grad.astype(jnp.bfloat16)
    grad_inner = weight_grad(normalized_input, inner_own)
    grad_step = weight_grad(normalized_input, step_grad)
    delta = jnp.sum(attended_grad.astype(jnp.float32) * attended_float, axis=-1).transpose(0, 2, 1)

    def make_back_pass():

        def back_pass(index, carry):
            query_grad, keyvalue_grad = carry
            keys, values, key_pos = key_piece(index)
            scores = block_scores(queries, keys, query_pos, key_pos, factor)
            probs = jnp.exp(scores - log_total[..., None])
            probs_grad = jnp.einsum(
                "sqhd,skd->shqk", attended_grad, values, preferred_element_type=jnp.float32
            )
            scores_grad = (probs * (probs_grad - delta[..., None])).astype(jnp.bfloat16)
            query_grad = (
                query_grad
                + jnp.einsum(
                    "shqk,skd->sqhd", scores_grad, keys, preferred_element_type=jnp.float32
                )
                * factor
            )
            key_grad = (
                jnp.einsum(
                    "shqk,sqhd->skd", scores_grad, queries, preferred_element_type=jnp.float32
                )
                * factor
            )
            value_grad = jnp.einsum(
                "shqk,sqhd->skd",
                probs.astype(jnp.bfloat16),
                attended_grad,
                preferred_element_type=jnp.float32,
            )
            keyvalue_grad = lax.dynamic_update_slice_in_dim(
                keyvalue_grad,
                jnp.concatenate([key_grad, value_grad], axis=-1),
                index * key_block,
                1,
            )
            return (query_grad, keyvalue_grad)

        return back_pass

    query_zero = jnp.zeros((sequences, rows, heads_here, head_dim), jnp.float32)
    keyvalue_zero = jnp.zeros((sequences, length, 2 * head_dim), jnp.float32)
    query_grad, keyvalue_grad_all = lax.fori_loop(
        0, blocks_needed, make_back_pass(), (query_zero, keyvalue_zero)
    )
    keyvalue_grad_own = summed_rows(keyvalue_grad_all, "seq")
    key_raw_grad = rotate(keyvalue_grad_own[:, :, None, :head_dim], -positions)[:, :, 0]
    keyvalue_raw_grad = jnp.concatenate([key_raw_grad, keyvalue_grad_own[..., head_dim:]], axis=-1)
    chooser = (jnp.arange(KV_HEADS, dtype=jnp.int32) == kv_index).astype(jnp.float32)
    keyvalue_both = chooser[None, None, :, None] * keyvalue_raw_grad[:, :, None, :]
    query_raw_grad = (
        rotate(query_grad, -positions)
        .astype(jnp.bfloat16)
        .reshape(sequences, rows, heads_here * head_dim)
    )
    grad_query = weight_grad(normalized_input, query_raw_grad)
    normed_part = (
        matmul_back(query_raw_grad, query_weight)
        + matmul_back(zgate_grad, zgate_weight)
        + matmul_back(inner_own, inner_weight)
        + matmul_back(step_grad, step_weight)
    )
    kv_width = keyvalue_both.shape[2] * keyvalue_both.shape[3]
    together = summed_rows(
        jnp.concatenate(
            [
                normed_part,
                keyvalue_both.reshape(sequences, rows, kv_width),
                inner_grad[..., inner_width:],
            ],
            axis=-1,
        ),
        "head",
    )
    normed_sum = together[..., :width]
    low_rows = together[..., width:].astype(jnp.bfloat16)
    shared_weight = jnp.concatenate(
        [keyvalue_matrix.reshape(width, kv_width), state_weight], axis=1
    )
    grad_shared = weight_grad(own_rows(normalized_input), low_rows)
    normed_grad = normed_sum + matmul_back(low_rows, shared_weight)
    norm_one_pull = jax.vjp(rms_norm, input_rows, gain_one)[1]
    input_norm_grad, grad_gain_one = norm_one_pull(normed_grad)
    input_rows_grad = (hidden_grad + input_norm_grad).astype(jnp.bfloat16)
    grad_input = lax.all_gather(input_rows_grad, "head", axis=1, tiled=True).astype(jnp.float32)
    own_small = [
        grad_step,
        conv_grad[:, :inner_width],
        grad_step_bias,
        grad_decay_log,
        grad_skip,
        grad_gain_ssm,
    ]
    all_small = [grad_gain_one, grad_gain_two, conv_grad[:, inner_width:]]

    plain = 2 * inner_width + grad_query.shape[1]
    last_share = summed_share(
        jnp.concatenate(
            [grad_zgate, grad_inner, grad_query, two_parts(own_small, width)], axis=1
        ),
        "seq",
    )
    last_sums = lax.all_gather(
        split_again(last_share, plain), "seq", axis=0, tiled=True
    ).astype(jnp.float32)
    shared_plain = grad_shared.shape[1]
    shared_part = split_again(
        summed_share(
            jnp.concatenate([grad_shared, two_parts(all_small, width)], axis=1), "head"
        ),
        shared_plain,
    )
    shared_part = split_again(summed_share(shared_part, "seq"), shared_plain)
    shared_sum = lax.all_gather(
        shared_part, ("head", "seq"), axis=0, tiled=True
    ).astype(jnp.float32)
    grad_step, conv_inner_grad, grad_step_bias, grad_decay_log, grad_skip, grad_gain_ssm = joined(
        last_sums[:, plain:], own_small
    )
    grad_gain_one, grad_gain_two, conv_state_grad = joined(
        shared_sum[:, shared_plain:], all_small
    )
    attended_width = heads_here * head_dim
    return (
        output,
        grad_input,
        grad_gain_one,
        last_sums[:, 2 * inner_width : plain],
        shared_sum[:, :kv_width].reshape(keyvalue_matrix.shape),
        mixed_sums[:attended_width],
        last_sums[:, :inner_width],
        last_sums[:, inner_width : 2 * inner_width],
        shared_sum[:, kv_width:shared_plain],
        grad_step,
        conv_inner_grad,
        conv_state_grad,
        grad_step_bias,
        grad_decay_log,
        grad_skip,
        grad_gain_ssm,
        mixed_sums[attended_width:],
        grad_gain_two,
        feed_sums[:, :units],
        feed_sums[:, units:],
        down_sum,
    )


def solution(mesh):
    placed = (
        P(None, "seq", None),
        P(),
        P(None, "head"),
        P(),
        P("head", None),
        P(None, "head"),
        P(None, "head"),
        P(),
        P(None, "head"),
        P(None, "head"),
        P(),
        P("head"),
        P("head"),
        P("head"),
        P("head"),
        P("head", None),
        P(),
        P(None, "head"),
        P(None, "head"),
        P("head", None),
        P(None, "seq", None),
    )
    return jax.shard_map(
        on_device,
        mesh=mesh,
        in_specs=placed,
        out_specs=(
            P(None, "seq", None),
            P(None, "seq", None),
            P(),
            P(None, "head"),
            P(),
            P("head", None),
            P(None, "head"),
            P(None, "head"),
            P(),
            P(None, "head"),
            P(None, "head"),
            P(),
            P("head"),
            P("head"),
            P("head"),
            P("head"),
            P("head", None),
            P(),
            P(None, "head"),
            P(None, "head"),
            P("head", None),
        ),
        check_vma=False,
    )
```

```python
import math

import jax
import jax.numpy as jnp
from jax import lax
from jax.sharding import PartitionSpec as P

HEADS = 8
KV_HEADS = 2
STATE = 128
SSM = 1536


HIGH_ACCURACY = lax.Precision.HIGHEST
EPSILON = 1e-05
ROPE_BASE = 100000000000.0
MASKED = -1e30


def passed_along(value, axis, steps):
    count = lax.axis_size(axis)
    first, last = (max(0, -steps), min(count, count - steps))
    return lax.ppermute(value, axis, [(source, source + steps) for source in range(first, last)])


def carried(log_totals, states, axis, backward):
    count, mine = (lax.axis_size(axis), lax.axis_index(axis))
    pieces = lax.all_gather(states.astype(jnp.bfloat16), axis)
    place = jnp.arange(count, dtype=jnp.int32)
    if backward:
        between = (place[None, :] < place[:, None]) & (place[None, :] > mine)
        used = place > mine
    else:
        between = (place[None, :] > place[:, None]) & (place[None, :] < mine)
        used = place < mine
    decay = jnp.sum(
        jnp.where(between[:, :, None, None], log_totals[None], 0.0), axis=1
    )
    weight = jnp.where(used[:, None, None], jnp.exp(decay), 0.0)
    return jnp.sum(weight[..., None, None] * pieces.astype(jnp.float32), axis=0)


def summed_share(value, axis):
    count = lax.axis_size(axis)
    pieces = value.astype(jnp.bfloat16).reshape(count, value.shape[0] // count, *value.shape[1:])
    landed = lax.all_to_all(pieces, axis, 0, 0)
    return jnp.sum(landed.astype(jnp.float32), axis=0)


def summed_rows(value, axis):
    count = lax.axis_size(axis)
    sequences, rows, width = value.shape
    pieces = value.astype(jnp.bfloat16).reshape(sequences, count, rows // count, width)
    landed = lax.all_to_all(pieces, axis, 1, 1)
    return jnp.sum(landed.astype(jnp.float32), axis=1)


def two_parts(values, rows):
    flat = jnp.concatenate([part.reshape(-1) for part in values])
    flat = jnp.pad(flat, (0, -flat.size % rows)).reshape(rows, -1)
    high = lax.reduce_precision(flat, 8, 7)
    return jnp.concatenate([high, flat - high], axis=1)


def joined(columns, likes):
    half = columns.shape[1] // 2
    flat = (columns[:, :half] + columns[:, half:]).reshape(-1)
    found, at = [], 0
    for like in likes:
        found.append(flat[at : at + like.size].reshape(like.shape))
        at += like.size
    return found


def split_again(share, plain):
    half = (share.shape[1] - plain) // 2
    flat = share[:, plain : plain + half] + share[:, plain + half :]
    high = lax.reduce_precision(flat, 8, 7)
    return jnp.concatenate([share[:, :plain], high, flat - high], axis=1).astype(jnp.bfloat16)


def early_share(value, axis):
    return lax.psum_scatter(
        value.astype(jnp.bfloat16), axis, scatter_dimension=0, tiled=True
    )


def gathered(share, axis):
    return lax.all_gather(share, axis, axis=0, tiled=True).astype(jnp.float32)


def matmul(left_operand, right_operand):
    return jnp.einsum(
        "std,de->ste", left_operand, right_operand, preferred_element_type=jnp.float32
    )


def matmul_back(grad, right_operand):
    return jnp.einsum("ste,de->std", grad, right_operand, preferred_element_type=jnp.float32)


def weight_grad(left_operand, grad):
    return jnp.einsum("std,ste->de", left_operand, grad, preferred_element_type=jnp.float32)


def rms_norm(values, gain):
    factor = lax.rsqrt(jnp.mean(values * values, axis=-1, keepdims=True) + EPSILON)
    return values * factor * gain


def rotate(values, positions):
    half = values.shape[-1] // 2
    freq = ROPE_BASE ** (-jnp.arange(half, dtype=jnp.float32) * 2.0 / values.shape[-1])
    angle = positions[:, None] * freq[None, :]
    cosine = jnp.cos(angle)[None, :, None, :]
    sine = jnp.sin(angle)[None, :, None, :]
    first = values[..., :half]
    second = values[..., half:]
    return jnp.concatenate(
        [first * cosine - second * sine, second * cosine + first * sine], axis=-1
    )


def block_scores(queries, keys, query_pos, key_pos, factor):
    scores = (
        jnp.einsum("sqhd,skd->shqk", queries, keys, preferred_element_type=jnp.float32) * factor
    )
    allowed = key_pos[None, :] <= query_pos[:, None]
    return jnp.where(allowed[None, None], scores, MASKED)


def conv_act(extended, conv_weight):
    rows = extended.shape[1] - (conv_weight.shape[0] - 1)
    summed = extended[:, 0:rows] * conv_weight[0]
    for tap in range(1, conv_weight.shape[0]):
        summed = summed + extended[:, tap : tap + rows] * conv_weight[tap]
    return jax.nn.silu(summed)


def ssm_inputs(extended, step_raw, conv_weight, step_bias, decay_log):
    activated = conv_act(extended, conv_weight)
    inner_width = activated.shape[-1] - 2 * STATE
    heads_here = step_raw.shape[-1]
    channels = activated[..., :inner_width].reshape(
        activated.shape[0], activated.shape[1], heads_here, inner_width // heads_here
    )
    writes = activated[..., inner_width : inner_width + STATE]
    reads = activated[..., inner_width + STATE :]
    step = jax.nn.softplus(step_raw + step_bias)
    logdecay = -step * jnp.exp(decay_log)
    return (channels, writes, reads, step, logdecay)


def intra(channels, writes, reads, step, running):
    rows = running.shape[1]
    lower = jnp.arange(rows, dtype=jnp.int32)[:, None] >= jnp.arange(rows, dtype=jnp.int32)[None, :]
    mask = lower[None, :, :, None]
    spread = running[:, :, None, :] - running[:, None, :, :]
    decay = jnp.where(mask, jnp.exp(jnp.where(mask, spread, 0.0)), 0.0)
    intersection = jnp.einsum("stn,sun->stu", reads, writes, precision=HIGH_ACCURACY)
    mixing = decay * intersection[..., None] * step[:, None, :, :]
    within = jnp.einsum("stuh,suhp->sthp", mixing, channels, precision=HIGH_ACCURACY)
    tail_weight = jnp.exp(running[:, -1:, :] - running) * step
    local = jnp.einsum("suh,suhp,sun->shpn", tail_weight, channels, writes, precision=HIGH_ACCURACY)
    return (within, local)


def inter(reads, running, state):
    return jnp.exp(running)[..., None] * jnp.einsum(
        "stn,shpn->sthp", reads, state, precision=HIGH_ACCURACY
    )


def ssm_full(extended, step_raw, conv_weight, step_bias, decay_log, skip_gain, state_in):
    channels, writes, reads, step, logdecay = ssm_inputs(
        extended, step_raw, conv_weight, step_bias, decay_log
    )
    running = running_sum(logdecay)
    within, local = intra(channels, writes, reads, step, running)
    result = within + inter(reads, running, state_in) + skip_gain[:, None] * channels
    state_end = jnp.exp(running[:, -1])[:, :, None, None] * state_in + local
    return (result, state_end)


def running_sum(values):
    rows = values.shape[1]
    lower = jnp.arange(rows, dtype=jnp.int32)[:, None] >= jnp.arange(rows, dtype=jnp.int32)[None, :]
    return jnp.einsum(
        "tu,suh->sth", lower.astype(jnp.float32), values, precision=HIGH_ACCURACY
    )


def on_device(
    hidden_in,
    norm_gain,
    query_weight,
    keyvalue_matrix,
    output_weight,
    zgate_weight,
    inner_weight,
    state_weight,
    step_weight,
    conv_inner,
    conv_state,
    step_bias,
    decay_log,
    skip_gain,
    ssm_gain,
    mixer_weight,
    mlp_gain,
    gate_weight,
    up_weight,
    down_weight,
    grad_output,
):
    sequences, rows, width = hidden_in.shape
    head_dim = keyvalue_matrix.shape[2] // 2
    heads_here = query_weight.shape[1] // head_dim
    group = HEADS // KV_HEADS
    factor = head_dim ** (-0.5)
    inner_width = inner_weight.shape[1]
    mamba_here = step_bias.shape[0]
    seq_index = lax.axis_index("seq")
    head_index = lax.axis_index("head")
    query_pos = seq_index * rows + jnp.arange(rows, dtype=jnp.int32)
    positions = query_pos.astype(jnp.float32)
    input_float = hidden_in.astype(jnp.float32)
    gain_one = norm_gain.astype(jnp.float32)
    normalized_input = rms_norm(input_float, gain_one).astype(jnp.bfloat16)
    query_raw = matmul(normalized_input, query_weight).reshape(
        sequences, rows, heads_here, head_dim
    )
    queries = rotate(query_raw, positions).astype(jnp.bfloat16)
    kv_index = head_index * heads_here // group
    own_weight = lax.dynamic_index_in_dim(keyvalue_matrix, kv_index, 1, keepdims=False)
    keyvalue_projected = matmul(normalized_input, own_weight)
    keys_own = rotate(keyvalue_projected[:, :, None, :head_dim], positions)[:, :, 0]
    keyvalue_own = jnp.concatenate([keys_own, keyvalue_projected[..., head_dim:]], axis=-1).astype(
        jnp.bfloat16
    )
    keyvalue_all = lax.all_gather(keyvalue_own, "seq", axis=1, tiled=True)
    length = keyvalue_all.shape[1]
    key_block = math.gcd(length, 512)
    blocks_needed = ((seq_index + 1) * rows + key_block - 1) // key_block

    def key_piece(index):
        start = index * key_block
        piece = lax.dynamic_slice_in_dim(keyvalue_all, start, key_block, 1)
        return (
            piece[..., :head_dim],
            piece[..., head_dim:],
            start + jnp.arange(key_block, dtype=jnp.int32),
        )

    def first_pass(index, carry):
        peak, total = carry
        keys, values, key_pos = key_piece(index)
        scores = block_scores(queries, keys, query_pos, key_pos, factor)
        new_peak = jnp.maximum(peak, jnp.max(scores, axis=-1))
        total = total * jnp.exp(peak - new_peak) + jnp.sum(
            jnp.exp(scores - new_peak[..., None]), axis=-1
        )
        return (new_peak, total)

    start_peak = jnp.full((sequences, heads_here, rows), MASKED, jnp.float32)
    peak, total = lax.fori_loop(
        0, blocks_needed, first_pass, (start_peak, jnp.zeros_like(start_peak))
    )
    log_total = peak + jnp.log(total)

    def second_pass(index, summed):
        keys, values, key_pos = key_piece(index)
        scores = block_scores(queries, keys, query_pos, key_pos, factor)
        probs = jnp.exp(scores - log_total[..., None]).astype(jnp.bfloat16)
        return summed + jnp.einsum(
            "shqk,skd->sqhd", probs, values, preferred_element_type=jnp.float32
        )

    attended_float = lax.fori_loop(
        0,
        blocks_needed,
        second_pass,
        jnp.zeros((sequences, rows, heads_here, head_dim), jnp.float32),
    )
    attended = attended_float.astype(jnp.bfloat16).reshape(sequences, rows, heads_here * head_dim)
    zgate = matmul(normalized_input, zgate_weight)
    inner = jnp.concatenate(
        [matmul(normalized_input, inner_weight), matmul(normalized_input, state_weight)], axis=-1
    )
    step_raw = matmul(normalized_input, step_weight)
    conv_weight = jnp.concatenate([conv_inner, conv_state], axis=1).astype(jnp.float32)
    taps = conv_weight.shape[0]
    before = passed_along(inner[:, rows - (taps - 1) :], "seq", 1)
    extended = jnp.concatenate([before, inner], axis=1)
    channels, writes, reads, step, logdecay = ssm_inputs(
        extended, step_raw, conv_weight, step_bias, decay_log
    )
    running = running_sum(logdecay)
    within, local = intra(channels, writes, reads, step, running)
    log_totals = lax.all_gather(running[:, -1], "seq")
    state_in = carried(log_totals, local, "seq", False)
    y_ssm = within + inter(reads, running, state_in) + skip_gain[:, None] * channels
    y_flat = y_ssm.reshape(sequences, rows, inner_width)
    gated = y_flat * jax.nn.silu(zgate)
    squares = lax.psum(jnp.sum(gated * gated, axis=-1), "head")
    ssm_factor = lax.rsqrt(squares / SSM + EPSILON)[..., None]
    gain_ssm = ssm_gain.astype(jnp.float32)
    ssm_normed = (gated * ssm_factor * gain_ssm).astype(jnp.bfloat16)
    branch_part = matmul(attended, output_weight) + matmul(ssm_normed, mixer_weight)
    quarter = rows // lax.axis_size("head")
    mixed_rows = summed_rows(branch_part, "head")
    def own_rows(value):
        return lax.dynamic_slice_in_dim(value, head_index * quarter, quarter, 1)

    input_rows = own_rows(input_float)
    hidden_rows = input_rows + mixed_rows
    gain_two = mlp_gain.astype(jnp.float32)
    normed_two_rows = rms_norm(hidden_rows, gain_two).astype(jnp.bfloat16)
    normed_two = lax.all_gather(normed_two_rows, "head", axis=1, tiled=True)
    gate = matmul(normed_two, gate_weight)
    up = matmul(normed_two, up_weight)
    activated = (jax.nn.silu(gate) * up).astype(jnp.bfloat16)
    feed_part = matmul(activated, down_weight)
    feed_own = lax.psum_scatter(
        feed_part.astype(jnp.bfloat16), "head", scatter_dimension=1, tiled=True
    )
    act_grad = matmul_back(grad_output, down_weight)
    grad_down = weight_grad(activated, grad_output)
    gate_pull = jax.vjp(lambda gate_in, up_in: jax.nn.silu(gate_in) * up_in, gate, up)[1]
    gate_grad, up_grad = gate_pull(act_grad)
    gate_grad = gate_grad.astype(jnp.bfloat16)
    up_grad = up_grad.astype(jnp.bfloat16)
    grad_gate = weight_grad(normed_two, gate_grad)
    grad_up = weight_grad(normed_two, up_grad)
    normed_two_grad = summed_rows(
        matmul_back(gate_grad, gate_weight) + matmul_back(up_grad, up_weight), "head"
    )
    units = grad_down.shape[0]
    down_share = early_share(grad_down, "seq")
    feed_share = early_share(jnp.concatenate([grad_gate, grad_up], axis=1), "seq")
    norm_two_pull = jax.vjp(rms_norm, hidden_rows, gain_two)[1]
    hidden_norm_grad, grad_gain_two = norm_two_pull(normed_two_grad)
    hidden_grad = own_rows(grad_output).astype(jnp.float32) + hidden_norm_grad
    mixed_grad = lax.all_gather(
        hidden_grad.astype(jnp.bfloat16), "head", axis=1, tiled=True
    )
    grad_output_proj = weight_grad(attended, mixed_grad)
    attended_grad = (
        matmul_back(mixed_grad, output_weight)
        .astype(jnp.bfloat16)
        .reshape(sequences, rows, heads_here, head_dim)
    )
    grad_mixer = weight_grad(ssm_normed, mixed_grad)
    mixed_share = early_share(jnp.concatenate([grad_output_proj, grad_mixer], axis=0), "seq")
    ssm_normed_grad = matmul_back(mixed_grad, mixer_weight)
    weighted = ssm_normed_grad * gain_ssm
    inner_total = lax.psum(jnp.sum(weighted * gated, axis=-1), "head")
    gated_grad = weighted * ssm_factor - gated * ssm_factor**3 * inner_total[..., None] / SSM
    grad_gain_ssm = jnp.sum(ssm_normed_grad * gated * ssm_factor, axis=(0, 1))
    gated_pull = jax.vjp(lambda y_in, z_in: y_in * jax.nn.silu(z_in), y_flat, zgate)[1]
    y_grad, zgate_grad = gated_pull(gated_grad)
    zgate_grad = zgate_grad.astype(jnp.bfloat16)
    grad_zgate = weight_grad(normalized_input, zgate_grad)
    y_grad_heads = y_grad.reshape(sequences, rows, mamba_here, inner_width // mamba_here)
    own_state_grad = jnp.einsum(
        "sth,stn,sthp->shpn", jnp.exp(running), reads, y_grad_heads, precision=HIGH_ACCURACY
    )
    state_grad = carried(log_totals, own_state_grad, "seq", True)
    ssm_pull = jax.vjp(
        ssm_full, extended, step_raw, conv_weight, step_bias, decay_log, skip_gain, state_in
    )[1]
    extended_grad, step_raw_grad, conv_grad, grad_step_bias, grad_decay_log, grad_skip, unused = (
        ssm_pull((y_grad_heads, state_grad))
    )
    before_grad = passed_along(extended_grad[:, : taps - 1], "seq", -1)
    inner_grad = extended_grad[:, taps - 1 :] + jnp.pad(
        before_grad, ((0, 0), (rows - (taps - 1), 0), (0, 0))
    )
    inner_own = inner_grad[..., :inner_width].astype(jnp.bfloat16)
    step_grad = step_raw_grad.astype(jnp.bfloat16)
    grad_inner = weight_grad(normalized_input, inner_own)
    grad_step = weight_grad(normalized_input, step_grad)
    delta = jnp.sum(attended_grad.astype(jnp.float32) * attended_float, axis=-1).transpose(0, 2, 1)

    def make_back_pass():

        def back_pass(index, carry):
            query_grad, keyvalue_grad = carry
            keys, values, key_pos = key_piece(index)
            scores = block_scores(queries, keys, query_pos, key_pos, factor)
            probs = jnp.exp(scores - log_total[..., None])
            probs_grad = jnp.einsum(
                "sqhd,skd->shqk", attended_grad, values, preferred_element_type=jnp.float32
            )
            scores_grad = (probs * (probs_grad - delta[..., None])).astype(jnp.bfloat16)
            query_grad = (
                query_grad
                + jnp.einsum(
                    "shqk,skd->sqhd", scores_grad, keys, preferred_element_type=jnp.float32
                )
                * factor
            )
            key_grad = (
                jnp.einsum(
                    "shqk,sqhd->skd", scores_grad, queries, preferred_element_type=jnp.float32
                )
                * factor
            )
            value_grad = jnp.einsum(
                "shqk,sqhd->skd",
                probs.astype(jnp.bfloat16),
                attended_grad,
                preferred_element_type=jnp.float32,
            )
            keyvalue_grad = lax.dynamic_update_slice_in_dim(
                keyvalue_grad,
                jnp.concatenate([key_grad, value_grad], axis=-1),
                index * key_block,
                1,
            )
            return (query_grad, keyvalue_grad)

        return back_pass

    query_zero = jnp.zeros((sequences, rows, heads_here, head_dim), jnp.float32)
    keyvalue_zero = jnp.zeros((sequences, length, 2 * head_dim), jnp.float32)
    query_grad, keyvalue_grad_all = lax.fori_loop(
        0, blocks_needed, make_back_pass(), (query_zero, keyvalue_zero)
    )
    down_share, feed_share, mixed_share, feed_own, unused = lax.optimization_barrier(
        (down_share, feed_share, mixed_share, feed_own, query_grad)
    )
    output_own = (hidden_rows + feed_own.astype(jnp.float32)).astype(jnp.bfloat16)
    output = lax.all_gather(output_own, "head", axis=1, tiled=True)
    down_sum = gathered(down_share, "seq")
    feed_sums = gathered(feed_share, "seq")
    mixed_sums = gathered(mixed_share, "seq")
    keyvalue_grad_own = summed_rows(keyvalue_grad_all, "seq")
    key_raw_grad = rotate(keyvalue_grad_own[:, :, None, :head_dim], -positions)[:, :, 0]
    keyvalue_raw_grad = jnp.concatenate([key_raw_grad, keyvalue_grad_own[..., head_dim:]], axis=-1)
    chooser = (jnp.arange(KV_HEADS, dtype=jnp.int32) == kv_index).astype(jnp.float32)
    keyvalue_both = chooser[None, None, :, None] * keyvalue_raw_grad[:, :, None, :]
    query_raw_grad = (
        rotate(query_grad, -positions)
        .astype(jnp.bfloat16)
        .reshape(sequences, rows, heads_here * head_dim)
    )
    grad_query = weight_grad(normalized_input, query_raw_grad)
    normed_part = (
        matmul_back(query_raw_grad, query_weight)
        + matmul_back(zgate_grad, zgate_weight)
        + matmul_back(inner_own, inner_weight)
        + matmul_back(step_grad, step_weight)
    )
    kv_width = keyvalue_both.shape[2] * keyvalue_both.shape[3]
    together = summed_rows(
        jnp.concatenate(
            [
                normed_part,
                keyvalue_both.reshape(sequences, rows, kv_width),
                inner_grad[..., inner_width:],
            ],
            axis=-1,
        ),
        "head",
    )
    normed_sum = together[..., :width]
    low_rows = together[..., width:].astype(jnp.bfloat16)
    shared_weight = jnp.concatenate(
        [keyvalue_matrix.reshape(width, kv_width), state_weight], axis=1
    )
    grad_shared = weight_grad(own_rows(normalized_input), low_rows)
    normed_grad = normed_sum + matmul_back(low_rows, shared_weight)
    norm_one_pull = jax.vjp(rms_norm, input_rows, gain_one)[1]
    input_norm_grad, grad_gain_one = norm_one_pull(normed_grad)
    input_rows_grad = (hidden_grad + input_norm_grad).astype(jnp.bfloat16)
    grad_input = lax.all_gather(input_rows_grad, "head", axis=1, tiled=True).astype(jnp.float32)
    own_small = [
        grad_step,
        conv_grad[:, :inner_width],
        grad_step_bias,
        grad_decay_log,
        grad_skip,
        grad_gain_ssm,
    ]
    all_small = [grad_gain_one, grad_gain_two, conv_grad[:, inner_width:]]

    plain = 2 * inner_width + grad_query.shape[1]
    last_share = summed_share(
        jnp.concatenate(
            [grad_zgate, grad_inner, grad_query, two_parts(own_small, width)], axis=1
        ),
        "seq",
    )
    last_sums = lax.all_gather(
        split_again(last_share, plain), "seq", axis=0, tiled=True
    ).astype(jnp.float32)
    shared_plain = grad_shared.shape[1]
    shared_part = split_again(
        summed_share(
            jnp.concatenate([grad_shared, two_parts(all_small, width)], axis=1), "head"
        ),
        shared_plain,
    )
    shared_part = split_again(summed_share(shared_part, "seq"), shared_plain)
    shared_sum = lax.all_gather(
        shared_part, ("head", "seq"), axis=0, tiled=True
    ).astype(jnp.float32)
    grad_step, conv_inner_grad, grad_step_bias, grad_decay_log, grad_skip, grad_gain_ssm = joined(
        last_sums[:, plain:], own_small
    )
    grad_gain_one, grad_gain_two, conv_state_grad = joined(
        shared_sum[:, shared_plain:], all_small
    )
    attended_width = heads_here * head_dim
    return (
        output,
        grad_input,
        grad_gain_one,
        last_sums[:, 2 * inner_width : plain],
        shared_sum[:, :kv_width].reshape(keyvalue_matrix.shape),
        mixed_sums[:attended_width],
        last_sums[:, :inner_width],
        last_sums[:, inner_width : 2 * inner_width],
        shared_sum[:, kv_width:shared_plain],
        grad_step,
        conv_inner_grad,
        conv_state_grad,
        grad_step_bias,
        grad_decay_log,
        grad_skip,
        grad_gain_ssm,
        mixed_sums[attended_width:],
        grad_gain_two,
        feed_sums[:, :units],
        feed_sums[:, units:],
        down_sum,
    )


def solution(mesh):
    placed = (
        P(None, "seq", None),
        P(),
        P(None, "head"),
        P(),
        P("head", None),
        P(None, "head"),
        P(None, "head"),
        P(),
        P(None, "head"),
        P(None, "head"),
        P(),
        P("head"),
        P("head"),
        P("head"),
        P("head"),
        P("head", None),
        P(),
        P(None, "head"),
        P(None, "head"),
        P("head", None),
        P(None, "seq", None),
    )
    return jax.shard_map(
        on_device,
        mesh=mesh,
        in_specs=placed,
        out_specs=(
            P(None, "seq", None),
            P(None, "seq", None),
            P(),
            P(None, "head"),
            P(),
            P("head", None),
            P(None, "head"),
            P(None, "head"),
            P(),
            P(None, "head"),
            P(None, "head"),
            P(),
            P("head"),
            P("head"),
            P("head"),
            P("head"),
            P("head", None),
            P(),
            P(None, "head"),
            P(None, "head"),
            P("head", None),
        ),
        check_vma=False,
    )
```
